768 devices in a mesh: row: 96 (over z_lo, y, core), col: 8 (over z_hi, x).
Axes of the slice: x: 4, y: 8, z: 12 (z_hi: 2, z_lo: 6; z = z_hi * 6 + z_lo), core: 2. Of those that a mesh axis runs over, the one named last changes fastest.
Arguments:
- velocity: bfloat16 [3, 2304, 256, 128], P(None, 'row', 'col'), may hold values from -6 to 6
- host_owner: int32 [12288, 1], P(('row', 'col')), may hold values from 0 to 7; in each aligned block of 16 rows (0 to 15, 16 to 31, ...) at most 4 rows name the same one
- host_site: int32 [3, 12288], P(None, ('row', 'col')), may hold values from 0 to 116, as said below
- vertices: float32 [24576, 3, 642], P(('row', 'col')), may hold values from -9 to 9
- triangles: int32 [3, 1280], replicated, may hold values from 0 to 641
- neighbours: int32 [4, 12288], P(None, ('row', 'col')), may hold values from 0 to 15, as said below
Outputs:
- force_field: float32 [3, 2304, 256, 128], P(None, 'row', 'col')
- vertex_velocity: float32 [12288, 3, 642], P(('row', 'col'))
The draws below stay inside these ranges and needn't reach their ends.
Inputs may be any that keep to these rules, and one draw needn't show every extreme that they name: `host_owner`: among the 16 cells of one device, at most 4 have the same owner. `host_site`: row 0 lies in 0 to 23, row 1 in 0 to 31, row 2 in 12 to 116. `neighbours`: each entry names another cell of the same device by its position among that device's 16 cells, never the cell itself. `vertices`: slots that no cell names hold values that no output reads.
All inputs are finite; a program needn't handle non-finite values.
Results may differ from the reference program's by a relative error of at most 0.0026.
Values may be sent and summed in bfloat16 or wider, within the bound.
No kernel may reach another device: no remote copies, remote signals or barrier semaphores. Data moves between devices by JAX's collectives and lax.ppermute only.
A program may use at most 32 MiB of HBM per device.

```python
import math
import jax
import jax.numpy as jnp
import numpy as np
from jax import lax

BX = 24
BY = 32
NZ = 128
HOST = 16
BRICK = 24
HALF = 12
VERTS = 642
NTRI = 1280
NB = 4
CAP = 4
NX = 2304
NY = 256
CELLS = 12288
SLOTS = 24576
N_ROW = 96
N_COL = 8


def draw_host_site(key, part):
    key_x, key_y, key_z = jax.random.split(key, 3)
    along_x = jax.random.randint(key_x, (CELLS,), 0, BX)
    along_y = jax.random.randint(key_y, (CELLS,), 0, BY)
    along_z = jax.random.randint(key_z, (CELLS,), HALF, NZ - HALF + 1)
    along_x = along_x.at[0].set(0)
    along_z = along_z.at[0].set(NZ - HALF)
    return jnp.stack([along_x, along_y, along_z]).astype(jnp.int32)


def draw_neighbours(key, part):
    shift_by = jax.random.randint(key, (NB, CELLS), 1, HOST)
    local_ids = jnp.arange(CELLS, dtype=jnp.int32) % HOST
    return ((local_ids[None, :] + shift_by) % HOST).astype(jnp.int32)


def touch_ends(result, rng, low, top_value):
    dims = result.shape
    spot = [jax.random.randint(jax.random.fold_in(rng, axis), (), 0, dims[axis]) for axis in range(len(dims))]
    result = result.at[tuple(spot)].set(low)
    longest = dims.index(max(dims))
    spot[longest] = (spot[longest] + 1) % dims[longest]
    return result.at[tuple(spot)].set(top_value)


def steps_of(own_key, shape, cuts, low, top_value):
    def one(position, parts):
        heights = jax.random.uniform(jax.random.fold_in(jax.random.fold_in(own_key, 6), position), (parts,), jnp.float32, low / len(cuts), top_value / len(cuts))
        return jnp.repeat(jnp.exp(heights), shape[position] // parts).reshape((-1,) + (1,) * (len(shape) - position - 1))

    factor_of = one(*cuts[0])
    for cut in cuts[1:]:
        factor_of = factor_of * one(*cut)
    return factor_of


def routed_block(stream_key, own, number, rows, count, top, reach, skew):
    order = jax.random.permutation(stream_key, count)
    crowded, ordinary = load_shares(count, rows * top, reach, skew, True), load_shares(count, rows * top, reach, skew, False)
    places = jnp.arange(count)

    def named(tallies, offset_by):
        used = int((tallies > 0).sum())
        fixed = max(1, used // 4)
        shifted = fixed + (places - fixed + offset_by * (used - fixed)) % max(1, count - fixed)
        return jnp.zeros((count,), jnp.int32).at[order[jnp.where(places < fixed, places, shifted)]].set(jnp.asarray(tallies, jnp.int32))

    tallies = jnp.where(number % 4 == 0, named(crowded, number // 4), named(ordinary, number - number // 4 - 1))
    mixed = jax.random.permutation(jax.random.fold_in(own, 3), count)
    donor, sink = mixed[0:count // 2 * 2:2], mixed[1:count // 2 * 2:2]
    margin = jnp.minimum(tallies[donor] - 1, reach - tallies[sink]) // 2
    margin = jnp.where((donor == order[0]) | (sink == order[0]) | (tallies[sink] == 0), 0, jnp.maximum(margin, 0))
    shifted = jax.random.randint(jax.random.fold_in(own, 4), (count // 2,), 0, 1 << 20) % (margin + 1)
    tallies = tallies.at[donor].add(-shifted).at[sink].add(shifted)
    labels = jnp.searchsorted(jnp.cumsum(tallies), jnp.arange(rows * top), side="right").astype(jnp.int32)
    listing = labels.reshape(top, rows).T
    listing = listing[jax.random.permutation(jax.random.fold_in(own, 1), rows)]
    offset_by = jax.random.randint(jax.random.fold_in(own, 2), (rows, 1), 0, top)
    return jnp.take_along_axis(listing, (jnp.arange(top)[None, :] + offset_by) % top, axis=1)


def load_shares(number_of, total, limit, slope, full):
    weights = [(1 << 20) // math.isqrt(rank ** slope) + 1 for rank in range(1, number_of + 1)]
    largest = limit if full else min(limit, max(-(-total // number_of), total * weights[0] // sum(weights)))
    least = 1 if total - largest >= number_of - 1 else 0
    counts, surplus = [largest] + [least] * (number_of - 1), total - largest - least * (number_of - 1)
    while surplus > 0:
        candidates = [i for i in range(1, number_of) if counts[i] < largest] or [i for i in range(1, number_of) if counts[i] < limit]
        mass, remaining = sum([weights[i] for i in candidates]), surplus
        for i in candidates:
            addition = min(limit - counts[i], max(1, remaining * weights[i] // mass), surplus)
            counts[i] = counts[i] + addition
            surplus = surplus - addition
    return np.array(counts)


def centred(rng, shape, deviation, reach, pieces=(), kind=jnp.bfloat16):
    result = jax.random.normal(rng, shape, jnp.float32) * deviation
    if len(pieces) > 0:
        result = steps_of(rng, shape, pieces, -0.22, 0.18) * result
    return jnp.clip(result, min=-reach, max=reach).astype(kind)


def setup_inputs(seed: int = 0) -> dict:
    splits = jax.random.split(jax.random.key(seed), 7)
    velocity = centred(splits[0], (3, NX, NY, NZ), 1.0, 6.0, ((1, 96), (2, 8)))
    host_owner_keys = jax.random.split(jax.random.fold_in(splits[1], 1), CELLS // HOST)
    host_owner_turns = jax.random.permutation(jax.random.fold_in(splits[1], 3), CELLS // HOST)
    host_owner = jax.vmap(lambda own, number: routed_block(jax.random.fold_in(splits[1], 2), own, number, HOST, N_COL, 1, CAP, 2))(host_owner_keys, host_owner_turns).reshape((CELLS, 1))
    host_site = draw_host_site(jax.random.fold_in(splits[6], 71), 0)
    vertices = jnp.clip(jax.random.uniform(splits[3], (SLOTS, 3, VERTS), jnp.float32, -9.0, 9.0) * steps_of(splits[3], (SLOTS, 3, VERTS), ((0, 768),), -0.4, 0.0), -9.0, 9.0)
    triangles = touch_ends(jax.random.randint(splits[4], (3, NTRI), 0, VERTS), jax.random.fold_in(splits[4], 1), 0, VERTS - 1).astype(jnp.int32)
    neighbours = draw_neighbours(jax.random.fold_in(splits[6], 71), 0)
    return {"velocity": velocity, "host_owner": host_owner, "host_site": host_site, "vertices": vertices, "triangles": triangles, "neighbours": neighbours}


repel_strength = 160.0
repel_radius_sq = 64.0


def kernel_weights(coords):
    nodes = (jnp.arange(BRICK) - HALF).astype(jnp.float32)
    distance = coords[None, :] - nodes[:, None]
    inside = jnp.abs(distance) < 2.0
    return jnp.where(inside, 0.25 * (1.0 + jnp.cos(0.5 * math.pi * distance)), 0.0 * distance)


def membrane_cell(brick_data, positions, anchor, near_centers, triangles):
    weight_x = kernel_weights(positions[0])
    weight_y = kernel_weights(positions[1])
    weight_z = kernel_weights(positions[2])
    cross_yz = (weight_y[:, None, :] * weight_z[None, :, :]).reshape(BRICK * BRICK, -1).astype(jnp.bfloat16)
    projected = jnp.dot(brick_data.reshape(3 * BRICK, BRICK * BRICK), cross_yz, preferred_element_type=jnp.float32)
    velocity_at = jnp.sum(projected.reshape(3, BRICK, -1) * weight_x[None], axis=1)
    half_span = HALF - 3
    stiffness = 3.0 / half_span
    rest_sq = 2.0 * half_span * half_span
    forces = jnp.zeros_like(positions)
    for head_end, tail_end in ((0, 1), (1, 2), (2, 0)):
        start_ids = triangles[head_end]
        end_ids = triangles[tail_end]
        edge_vec = positions[:, end_ids] - positions[:, start_ids]
        stretch = stiffness * (jnp.sum(edge_vec * edge_vec, axis=0) / rest_sq - 1.0)
        forces = forces.at[:, start_ids].add(stretch * edge_vec)
        forces = forces.at[:, end_ids].add(-stretch * edge_vec)
    placed = anchor[:, None] + positions
    for neighbour in range(NB):
        offset_vec = placed - near_centers[neighbour][:, None]
        forces = forces + repel_strength * offset_vec / (repel_radius_sq + jnp.sum(offset_vec * offset_vec, axis=0))
    spread_in = (forces[:, None, :] * weight_x[None]).reshape(3 * BRICK, -1).astype(jnp.bfloat16)
    force_brick = lax.dot_general(spread_in, cross_yz, (((1,), (1,)), ((), ())), preferred_element_type=jnp.float32)
    return velocity_at, force_brick.reshape(3, BRICK, BRICK, BRICK)


def reference(velocity, host_owner, host_site, vertices, triangles, neighbours):
    devices_all = N_ROW * N_COL
    slot_count = N_COL * CAP
    owners = host_owner[:, 0].reshape(devices_all, HOST)
    matches = (owners[:, :, None] == jnp.arange(N_COL, dtype=jnp.int32)[None, None, :]).astype(jnp.int32)
    ranking = jnp.sum((jnp.cumsum(matches, axis=1) - 1) * matches, axis=2)
    device_ids = jnp.arange(devices_all, dtype=jnp.int32)[:, None]
    row_ids = device_ids // N_COL
    col_ids = device_ids % N_COL
    slot_ids = ((row_ids * N_COL + owners) * slot_count + col_ids * CAP + ranking).reshape(-1)
    cell_pos = vertices[slot_ids]
    lattice_x = (row_ids * BX + host_site[0].reshape(devices_all, HOST)).reshape(-1)
    lattice_y = (col_ids * BY + host_site[1].reshape(devices_all, HOST)).reshape(-1)
    corners_int = jnp.stack([lattice_x, lattice_y, host_site[2]], axis=1).astype(jnp.int32)
    anchors = corners_int.astype(jnp.float32)
    centroids = anchors + jnp.mean(cell_pos, axis=2)
    base_ids = (jnp.arange(CELLS, dtype=jnp.int32) // HOST) * HOST
    near_ids = base_ids[None, :] + neighbours
    near_centers = jnp.transpose(centroids[near_ids], (1, 0, 2))
    padded_velocity = jnp.pad(velocity, ((0, 0), (HALF, HALF), (HALF, HALF), (0, 0)))
    force_pad = jnp.zeros((3, NX + 2 * HALF, NY + 2 * HALF, NZ), jnp.float32)

    def advance(force_acc, inputs):
        corner, positions, anchor, centers = inputs
        start = (jnp.int32(0), corner[0], corner[1], corner[2] - HALF)
        brick_data = lax.dynamic_slice(padded_velocity, start, (3, BRICK, BRICK, BRICK))
        velocity_at, force_brick = membrane_cell(brick_data, positions, anchor, centers, triangles)
        current = lax.dynamic_slice(force_acc, start, (3, BRICK, BRICK, BRICK))
        force_acc = lax.dynamic_update_slice(force_acc, current + force_brick, start)
        return force_acc, velocity_at

    force_pad, velocities = lax.scan(advance, force_pad, (corners_int, cell_pos, anchors, near_centers))
    return force_pad[:, HALF:HALF + NX, HALF:HALF + NY, :], velocities
```

```python
import math

import jax
import jax.numpy as jnp
from jax import lax
from jax.sharding import PartitionSpec as P

BRICK = 24
HALF = 12
NB = 4


repel_strength = 160.0
repel_radius_sq = 64.0


def extended_2(cells, sides, width):
    for axis, dim in sides:
        count = lax.axis_size(axis)
        ends = count - 1
        head = lax.slice_in_dim(cells, 0, width, axis=dim)
        tail = lax.slice_in_dim(cells, cells.shape[dim] - width, cells.shape[dim], axis=dim)
        cells = jnp.concatenate(
            [
                lax.ppermute(tail, axis, [(i, (i + 1) % count) for i in range(ends)]),
                cells,
                lax.ppermute(head, axis, [((i + 1) % count, i) for i in range(ends)]),
            ],
            axis=dim,
        )
    return cells


def kernel_weights(coords):
    nodes = (jnp.arange(BRICK) - HALF).astype(jnp.float32)
    distance = coords[None, :] - nodes[:, None]
    inside = jnp.abs(distance) < 2.0
    return jnp.where(inside, 0.25 * (1.0 + jnp.cos(0.5 * math.pi * distance)), 0.0 * distance)


def elastic_all(cell_pos, triangles):
    hosted = cell_pos.shape[0]
    vert_count = cell_pos.shape[2]
    tri_count = triangles.shape[1]
    half_span = HALF - 3
    stiffness = 3.0 / half_span
    rest_sq = 2.0 * half_span * half_span
    vert_ids = jnp.arange(vert_count, dtype=jnp.int32)
    corner_tables = [
        (triangles[k][None, :] == vert_ids[:, None]).astype(jnp.float32) for k in range(3)
    ]
    flat_pos = cell_pos.reshape(hosted * 3, vert_count)
    forces = jnp.zeros((hosted * 3, vert_count), jnp.float32)
    for head_end, tail_end in ((0, 1), (1, 2), (2, 0)):
        incidence = corner_tables[tail_end] - corner_tables[head_end]
        edge_vec = jnp.dot(flat_pos, incidence, precision=lax.Precision.HIGHEST).reshape(
            hosted, 3, tri_count
        )
        stretch = stiffness * (jnp.sum(edge_vec * edge_vec, axis=1) / rest_sq - 1.0)
        pushed = (stretch[:, None, :] * edge_vec).reshape(hosted * 3, tri_count)
        forces = forces - lax.dot_general(
            pushed, incidence, (((1,), (1,)), ((), ())), precision=lax.Precision.HIGHEST
        )
    return forces.reshape(hosted, 3, vert_count)


def membrane_cell(brick_data, positions, elastic, anchor, near_centers):
    weight_x = kernel_weights(positions[0])
    weight_y = kernel_weights(positions[1])
    weight_z = kernel_weights(positions[2])
    cross_yz = (
        (weight_y[:, None, :] * weight_z[None, :, :])
        .reshape(BRICK * BRICK, -1)
        .astype(jnp.bfloat16)
    )
    projected = jnp.dot(
        brick_data.reshape(3 * BRICK, BRICK * BRICK), cross_yz, preferred_element_type=jnp.float32
    )
    velocity_at = jnp.sum(projected.reshape(3, BRICK, -1) * weight_x[None], axis=1)
    forces = elastic
    placed = anchor[:, None] + positions
    for neighbour in range(NB):
        offset_vec = placed - near_centers[neighbour][:, None]
        forces = forces + repel_strength * offset_vec / (
            repel_radius_sq + jnp.sum(offset_vec * offset_vec, axis=0)
        )
    spread_in = (forces[:, None, :] * weight_x[None]).reshape(3 * BRICK, -1).astype(jnp.bfloat16)
    force_brick = lax.dot_general(
        spread_in, cross_yz, (((1,), (1,)), ((), ())), preferred_element_type=jnp.float32
    )
    return (velocity_at, force_brick)


def fold_margins(padded, dim, inner):
    lower_rim = lax.slice_in_dim(padded, 0, HALF, axis=dim)
    center_part = lax.slice_in_dim(padded, 2 * HALF, 2 * HALF + inner, axis=dim)
    upper_rim = lax.slice_in_dim(padded, inner + 3 * HALF, inner + 4 * HALF, axis=dim)
    widths_low = [(0, 0)] * padded.ndim
    widths_low[dim] = (0, inner - HALF)
    widths_up = [(0, 0)] * padded.ndim
    widths_up[dim] = (inner - HALF, 0)
    return center_part + jnp.pad(lower_rim, widths_low) + jnp.pad(upper_rim, widths_up)


def on_device(velocity, host_owner, host_site, vertices, triangles, neighbours):
    column_count = lax.axis_size("col")
    slot_total = vertices.shape[0]
    capacity = slot_total // column_count
    hosted = host_owner.shape[0]
    block_x = velocity.shape[1]
    block_y = velocity.shape[2]
    depth = velocity.shape[3]
    row_padded = extended_2(velocity, (("row", 1),), HALF)
    extended = extended_2(row_padded, (("col", 2),), HALF)
    arrived = lax.all_to_all(vertices, "col", split_axis=0, concat_axis=0, tiled=True)
    owners = host_owner[:, 0]
    earlier = jnp.arange(hosted)[None, :] < jnp.arange(hosted)[:, None]
    ranking = jnp.sum(
        ((owners[:, None] == owners[None, :]) & earlier).astype(jnp.int32), axis=1
    )
    picked = owners * capacity + ranking
    slot_select = (picked[:, None] == jnp.arange(slot_total, dtype=jnp.int32)[None, :]).astype(
        jnp.float32
    )
    cell_pos = jnp.einsum("qs,smv->qmv", slot_select, arrived, precision=lax.Precision.HIGHEST)
    elastic = elastic_all(cell_pos, triangles)
    lattice_x = lax.axis_index("row") * block_x + host_site[0]
    lattice_y = lax.axis_index("col") * block_y + host_site[1]
    corners_int = jnp.stack([lattice_x, lattice_y, host_site[2]], axis=1)
    anchors = corners_int.astype(jnp.float32)
    centroids = anchors + jnp.mean(cell_pos, axis=2)
    selector = (
        neighbours[:, :, None] == jnp.arange(hosted, dtype=jnp.int32)[None, None, :]
    ).astype(jnp.float32)
    near_centers = jnp.einsum("nqk,kc->qnc", selector, centroids, precision=lax.Precision.HIGHEST)
    local_corner = jnp.stack([host_site[0], host_site[1], host_site[2] - HALF], axis=1)
    force_ext = jnp.zeros((3, block_x + 2 * HALF, block_y + 2 * HALF, depth), jnp.float32)
    depth_ids = jnp.arange(depth, dtype=jnp.int32)
    brick_ids = jnp.arange(BRICK, dtype=jnp.int32)

    def advance(force_acc, inputs):
        corner, positions, elastic_here, anchor, centers = inputs
        start = (jnp.int32(0), corner[0], corner[1], corner[2])
        brick_data = lax.dynamic_slice(extended, start, (3, BRICK, BRICK, BRICK))
        velocity_at, force_brick = membrane_cell(
            brick_data, positions, elastic_here, anchor, centers
        )
        depth_place = (depth_ids[None, :] == corner[2] + brick_ids[:, None]).astype(jnp.float32)
        widened = jnp.dot(
            force_brick.reshape(3 * BRICK * BRICK, BRICK),
            depth_place,
            precision=lax.Precision.HIGHEST,
        )
        column_start = (jnp.int32(0), corner[0], corner[1], jnp.int32(0))
        current = lax.dynamic_slice(force_acc, column_start, (3, BRICK, BRICK, depth))
        force_acc = lax.dynamic_update_slice(
            force_acc, current + widened.reshape(3, BRICK, BRICK, depth), column_start
        )
        return (force_acc, velocity_at)

    force_ext, velocities = lax.scan(
        advance, force_ext, (local_corner, cell_pos, elastic, anchors, near_centers)
    )
    rows_padded = extended_2(force_ext, (("row", 1),), HALF)
    folded_rows = fold_margins(rows_padded, 1, block_x)
    cols_padded = extended_2(folded_rows, (("col", 2),), HALF)
    force_field = fold_margins(cols_padded, 2, block_y)
    return (force_field, velocities)


def solution(mesh):
    return jax.shard_map(
        on_device,
        mesh=mesh,
        in_specs=(
            P(None, "row", "col", None),
            P(("row", "col"), None),
            P(None, ("row", "col")),
            P(("row", "col"), None, None),
            P(),
            P(None, ("row", "col")),
        ),
        out_specs=(P(None, "row", "col", None), P(("row", "col"), None, None)),
        check_vma=False,
    )
```

```python
import functools
import math

import jax
import jax.numpy as jnp
from jax import lax
from jax.experimental import pallas as pl
from jax.experimental.pallas import tpu as pltpu
from jax.sharding import PartitionSpec as P

BRICK = 24
HALF = 12
NB = 4
LANES = 128
SLOT = 32
PER_TILE = LANES // SLOT
GROUPS = BRICK // PER_TILE
TRI_CHUNK = 256
FAR = 64.0

repel_strength = 160.0
repel_radius_sq = 64.0

F32 = jnp.float32
BF16 = jnp.bfloat16
VMEM_LIMIT = 48 * 1024 * 1024


def padded_to(size, multiple):
    return -(-size // multiple) * multiple


def rims(cells, axis, dim, width):
    count = lax.axis_size(axis)
    ends = count - 1
    head = lax.slice_in_dim(cells, 0, width, axis=dim)
    tail = lax.slice_in_dim(cells, cells.shape[dim] - width, cells.shape[dim], axis=dim)
    return from_previous(tail, axis, ends, count), from_next(head, axis, ends, count)


def from_previous(value, axis, ends, count):
    return lax.ppermute(value, axis, [(i, (i + 1) % count) for i in range(ends)])


def from_next(value, axis, ends, count):
    return lax.ppermute(value, axis, [((i + 1) % count, i) for i in range(ends)])


def node_weights(p, c, s, rows):
    lanes = p.shape[1]
    r = lax.broadcasted_iota(jnp.int32, (8, lanes), 0)
    base = jnp.where(r % 2 == 1, s, c)
    pattern = 0.25 * (1.0 + jnp.where(r % 4 >= 2, -base, base))
    nodes = (r - HALF).astype(F32)
    parts = []
    for block in range(rows // 8):
        distance = p - (nodes + 8.0 * block)
        parts.append(jnp.where(jnp.abs(distance) < 2.0, pattern, 0.0))
    return jnp.concatenate(parts, axis=0)


def cell_weights(posc, q, wyz):
    row = lambda kind: posc[kind, pl.ds(q, 1), :]
    wx, wy, wz = (node_weights(row(a), row(3 + a), row(6 + a), BRICK) for a in range(3))
    empty = jnp.zeros((SLOT - BRICK, wz.shape[1]), F32)
    for j in range(BRICK):
        wyz[SLOT * j : SLOT * (j + 1), :] = jnp.concatenate(
            [wy[j : j + 1] * wz, empty], axis=0
        ).astype(BF16)
    return wx


def split3(x):
    hi = x.astype(BF16)
    rest = x - hi.astype(F32)
    mid = rest.astype(BF16)
    return hi, mid, (rest - mid.astype(F32)).astype(BF16)


def spread_kernel(
    pitch_x, pitch_y, meta, arrived, anchors, select, triangles,
    posc, low, up, center, field, wyz, force,
):
    hosted = posc.shape[1]
    lanes = posc.shape[2]
    verts = arrived.shape[2]
    block_x = center.shape[1]

    field[...] = jnp.zeros_like(field)
    posc[0:3] = jnp.full((3, hosted, lanes), FAR, F32)
    for q in range(hosted):
        for a in range(3):
            posc[a, q : q + 1, 0:verts] = arrived[meta[0, q], a : a + 1, :]
    for a in range(3):
        p = posc[a]
        turned = (0.5 * math.pi) * (p - 4.0 * jnp.floor(0.25 * p + 0.5))
        posc[3 + a] = jnp.cos(turned)
        posc[6 + a] = jnp.sin(turned)

    pos = posc[0:3]
    flat = pos.reshape(3 * hosted, lanes)
    parts = jnp.concatenate(split3(flat), axis=0)
    rows = 3 * hosted
    half_span = HALF - 3
    stiffness = 3.0 / half_span
    rest_sq = 2.0 * half_span * half_span
    ids = lax.broadcasted_iota(jnp.int32, (lanes, TRI_CHUNK), 0)

    def chunk(t, acc):
        at = pl.multiple_of(t * TRI_CHUNK, TRI_CHUNK)
        tables = []
        corners = []
        for k in range(3):
            hit = ids == triangles[k : k + 1, pl.ds(at, TRI_CHUNK)]
            table = jnp.where(hit, 1.0, 0.0).astype(BF16)
            got = jnp.dot(parts, table, preferred_element_type=F32)
            tables.append(table)
            corners.append(got[0:rows] + got[rows : 2 * rows] + got[2 * rows : 3 * rows])
        pushes = []
        for k in range(3):
            edge = corners[(k + 1) % 3] - corners[k]
            e = edge.reshape(3, hosted, TRI_CHUNK)
            stretch = stiffness * (jnp.sum(e * e, axis=0) / rest_sq - 1.0)
            pushes.append((stretch[None] * e).reshape(rows, TRI_CHUNK))
        for k in range(3):
            net = pushes[k] - pushes[(k + 2) % 3]
            hi = net.astype(BF16)
            lo = (net - hi.astype(F32)).astype(BF16)
            acc = acc + lax.dot_general(
                jnp.concatenate([hi, lo], axis=0), tables[k],
                (((1,), (1,)), ((), ())), preferred_element_type=F32,
            )
        return acc

    chunks = triangles.shape[1] // TRI_CHUNK
    acc = lax.fori_loop(0, chunks, chunk, jnp.zeros((2 * rows, lanes), F32))
    force[...] = (acc[0:rows] + acc[rows:]).reshape(3, hosted, lanes)

    lane_ids = lax.broadcasted_iota(jnp.int32, (hosted, lanes), 1)
    square = lax.broadcasted_iota(jnp.int32, (hosted, hosted), 0) == lax.broadcasted_iota(
        jnp.int32, (hosted, hosted), 1
    )
    centres = []
    for a in range(3):
        mean = jnp.sum(jnp.where(lane_ids < verts, posc[a], 0.0), axis=1, keepdims=True) / verts
        column = anchors[a] + mean
        centres.append(jnp.sum(jnp.where(square, column, 0.0), axis=0, keepdims=True))
    for l in range(NB):
        offset = []
        for a in range(3):
            near = jnp.sum(jnp.where(select[l] > 0.5, centres[a], 0.0), axis=1, keepdims=True)
            offset.append((anchors[a] + posc[a]) - near)
        size_sq = offset[0] * offset[0] + offset[1] * offset[1] + offset[2] * offset[2]
        scale = repel_strength / (repel_radius_sq + size_sq)
        for a in range(3):
            force[a] += offset[a] * scale

    lane = lax.broadcasted_iota(jnp.int32, (BRICK, LANES), 1)

    def cell(q, carry):
        wx = cell_weights(posc, q, wyz)
        spread = jnp.concatenate(
            [force[a, pl.ds(q, 1), :] * wx for a in range(3)], axis=0
        ).astype(BF16)
        brick = lax.dot_general(
            spread, wyz[...], (((1,), (1,)), ((), ())), preferred_element_type=F32
        )
        z0 = meta[3, q]
        first = meta[1, q] * pitch_y + meta[2, q] + 4
        inside = (lane >= z0) & (lane < z0 + BRICK)
        for g in range(GROUPS):
            tile = brick[:, LANES * g : LANES * (g + 1)]
            for s in range(PER_TILE):
                turned = pltpu.roll(tile, lax.rem(z0 + LANES - SLOT * s, LANES), 1)
                for a in range(3):
                    here = pl.ds(
                        first + a * pitch_x * pitch_y + PER_TILE * g + s, BRICK, stride=pitch_y
                    )
                    field[here, :] += jnp.where(
                        inside, turned[BRICK * a : BRICK * (a + 1)], 0.0
                    )
        return carry

    lax.fori_loop(0, hosted, cell, 0)

    tall = low.shape[2]
    for a in range(3):

        def rim(x, carry):
            at = (a * pitch_x + x) * pitch_y
            low[a, x] = field[pl.ds(at, tall), :].astype(low.dtype)
            top = at + (HALF + block_x) * pitch_y
            up[a, x] = field[pl.ds(top, tall), :].astype(up.dtype)
            return carry

        def middle(x, carry):
            center[a, x] = field[pl.ds((a * pitch_x + HALF + x) * pitch_y, tall), :]
            return carry

        lax.fori_loop(0, HALF, rim, 0)
        lax.fori_loop(0, block_x, middle, 0)


def gather_kernel(
    pitch_x, pitch_y, meta, posc, own, row_low, row_up, col_low, col_up, out, lattice, wyz
):
    hosted = posc.shape[1]
    verts = out.shape[2]
    block_x, block_y = own.shape[1], own.shape[2]

    for a in range(3):

        def inner(x, carry):
            at = (a * pitch_x + HALF + x) * pitch_y + HALF
            lattice[pl.ds(at, block_y), :] = own[a, x].astype(F32)
            return carry

        def row_rim(x, carry):
            at = (a * pitch_x + x) * pitch_y + HALF
            lattice[pl.ds(at, block_y), :] = row_low[a, x].astype(F32)
            top = at + (HALF + block_x) * pitch_y
            lattice[pl.ds(top, block_y), :] = row_up[a, x].astype(F32)
            return carry

        def col_rim(x, carry):
            at = (a * pitch_x + x) * pitch_y
            lattice[pl.ds(at, HALF), :] = col_low[a, x].astype(F32)
            lattice[pl.ds(at + HALF + block_y, HALF), :] = col_up[a, x].astype(F32)
            return carry

        lax.fori_loop(0, block_x, inner, 0)
        lax.fori_loop(0, HALF, row_rim, 0)
        lax.fori_loop(0, block_x + 2 * HALF, col_rim, 0)

    slot_of = lax.broadcasted_iota(jnp.int32, (3 * BRICK, LANES), 1) // SLOT

    def cell(q, carry):
        wx = cell_weights(posc, q, wyz)
        z0 = meta[3, q]
        first = meta[1, q] * pitch_y + meta[2, q]
        tiles = []
        for g in range(GROUPS):
            tile = None
            for s in range(PER_TILE):
                lines = jnp.concatenate(
                    [
                        lattice[
                            pl.ds(
                                first + a * pitch_x * pitch_y + PER_TILE * g + s,
                                BRICK,
                                stride=pitch_y,
                            ),
                            :,
                        ]
                        for a in range(3)
                    ],
                    axis=0,
                )
                turned = pltpu.roll(lines, lax.rem(LANES + SLOT * s - z0, LANES), 1)
                tile = turned if tile is None else jnp.where(slot_of == s, turned, tile)
            tiles.append(tile.astype(BF16))
        brick = jnp.concatenate(tiles, axis=1)
        projected = jnp.dot(brick, wyz[...], preferred_element_type=F32)
        found = jnp.sum(projected.reshape(3, BRICK, -1) * wx[None], axis=1)
        out[q] = found[:, 0:verts]
        return carry

    lax.fori_loop(0, hosted, cell, 0)


def on_device(velocity, host_owner, host_site, vertices, triangles, neighbours):
    columns = lax.axis_size("col")
    rows = lax.axis_size("row")
    capacity = vertices.shape[0] // columns
    verts = vertices.shape[2]
    lanes = padded_to(verts, LANES)
    hosted = host_owner.shape[0]
    block_x, block_y, depth = velocity.shape[1:]
    wide_x, wide_y = block_x + 2 * HALF, block_y + 2 * HALF

    arrived = lax.all_to_all(vertices, "col", split_axis=0, concat_axis=0, tiled=True)
    row_low, row_up = rims(velocity, "row", 1, HALF)
    row_padded = jnp.concatenate([row_low, velocity, row_up], axis=1)
    col_low, col_up = rims(row_padded, "col", 2, HALF)

    owners = host_owner[:, 0]
    ids = jnp.arange(hosted, dtype=jnp.int32)
    earlier = ids[None, :] < ids[:, None]
    ranking = jnp.sum(
        ((owners[:, None] == owners[None, :]) & earlier).astype(jnp.int32), axis=1
    )
    picked = owners * capacity + ranking
    meta = jnp.stack([picked, host_site[0], host_site[1], host_site[2] - HALF])
    origin = jnp.stack(
        [lax.axis_index("row") * block_x, lax.axis_index("col") * block_y, jnp.int32(0)]
    ).astype(jnp.int32)
    anchors = (host_site + origin[:, None]).astype(F32)[:, :, None]
    select = (neighbours[:, :, None] == ids[None, None, :]).astype(F32)

    smem = pl.BlockSpec(memory_space=pltpu.SMEM)
    vmem = pl.BlockSpec(memory_space=pltpu.VMEM)
    tall = block_y + 2 * (HALF + 4)
    field_pitch = tall + 1
    posc, low, up, center = pl.pallas_call(
        functools.partial(spread_kernel, wide_x, field_pitch),
        out_shape=(
            jax.ShapeDtypeStruct((9, hosted, lanes), F32),
            jax.ShapeDtypeStruct((3, HALF, tall, depth), BF16),
            jax.ShapeDtypeStruct((3, HALF, tall, depth), BF16),
            jax.ShapeDtypeStruct((3, block_x, tall, depth), F32),
        ),
        in_specs=[smem, vmem, vmem, vmem, vmem],
        out_specs=(vmem, vmem, vmem, vmem),
        scratch_shapes=[
            pltpu.VMEM((3 * wide_x * field_pitch, depth), F32),
            pltpu.VMEM((SLOT * BRICK, lanes), BF16),
            pltpu.VMEM((3, hosted, lanes), F32),
        ],
        compiler_params=pltpu.CompilerParams(vmem_limit_bytes=VMEM_LIMIT),
        name="spread_forces",
    )(meta, arrived, anchors, select, triangles)

    up_in = from_previous(up, "row", rows - 1, rows)
    low_in = from_next(low, "row", rows - 1, rows)

    lattice_pitch = padded_to(wide_y, 8) + 1
    velocities = pl.pallas_call(
        functools.partial(gather_kernel, wide_x, lattice_pitch),
        out_shape=jax.ShapeDtypeStruct((hosted, 3, verts), F32),
        in_specs=[smem, vmem, vmem, vmem, vmem, vmem, vmem],
        out_specs=vmem,
        scratch_shapes=[
            pltpu.VMEM((3 * wide_x * lattice_pitch, depth), F32),
            pltpu.VMEM((SLOT * BRICK, lanes), BF16),
        ],
        compiler_params=pltpu.CompilerParams(vmem_limit_bytes=VMEM_LIMIT),
        name="interpolate_velocity",
    )(meta, posc, velocity, row_low, row_up, col_low, col_up)

    folded = center + jnp.concatenate([up_in, low_in], axis=1).astype(F32)
    edge = HALF + 4
    left = folded[:, :, 0:edge].astype(BF16)
    right = folded[:, :, edge + block_y :].astype(BF16)
    right_in = from_previous(right, "col", columns - 1, columns)
    left_in = from_next(left, "col", columns - 1, columns)
    force_field = folded[:, :, edge : edge + block_y] + jnp.concatenate(
        [right_in, left_in], axis=2
    ).astype(F32)
    return (force_field, velocities)


def solution(mesh):
    return jax.shard_map(
        on_device,
        mesh=mesh,
        in_specs=(
            P(None, "row", "col", None),
            P(("row", "col"), None),
            P(None, ("row", "col")),
            P(("row", "col"), None, None),
            P(),
            P(None, ("row", "col")),
        ),
        out_specs=(P(None, "row", "col", None), P(("row", "col"), None, None)),
        check_vma=False,
    )
```

```python
import functools
import math

import jax
import jax.numpy as jnp
from jax import lax
from jax.experimental import pallas as pl
from jax.experimental.pallas import tpu as pltpu
from jax.sharding import PartitionSpec as P

BRICK = 24
HALF = 12
NB = 4
LANES = 128
SLOT = 32
PER_TILE = LANES // SLOT
GROUPS = BRICK // PER_TILE
TRI_CHUNK = 256
TOGETHER = 4
FAR = 64.0

repel_strength = 160.0
repel_radius_sq = 64.0

F32 = jnp.float32
BF16 = jnp.bfloat16
VMEM_LIMIT = 48 * 1024 * 1024


def padded_to(size, multiple):
    return -(-size // multiple) * multiple


def from_previous(value, axis, ends, count):
    return lax.ppermute(value, axis, [(i, (i + 1) % count) for i in range(ends)])


def from_next(value, axis, ends, count):
    return lax.ppermute(value, axis, [((i + 1) % count, i) for i in range(ends)])


def node_weights(p, c, s, rows):
    lanes = p.shape[1]
    r = lax.broadcasted_iota(jnp.int32, (8, lanes), 0)
    base = jnp.where(r % 2 == 1, s, c)
    pattern = 0.25 * (1.0 + jnp.where(r % 4 >= 2, -base, base))
    nodes = (r - HALF).astype(F32)
    parts = []
    for block in range(rows // 8):
        distance = p - (nodes + 8.0 * block)
        parts.append(jnp.where(jnp.abs(distance) < 2.0, pattern, 0.0))
    return jnp.concatenate(parts, axis=0)


def cell_weights(posc, q, wyz):
    row = lambda kind: posc[kind, pl.ds(q, 1), :]
    wx, wy, wz = (node_weights(row(a), row(3 + a), row(6 + a), BRICK) for a in range(3))
    empty = jnp.zeros((SLOT - BRICK, wz.shape[1]), F32)
    for j in range(BRICK):
        wyz[SLOT * j : SLOT * (j + 1), :] = jnp.concatenate(
            [wy[j : j + 1] * wz, empty], axis=0
        ).astype(BF16)
    return wx


def split3(x):
    hi = x.astype(BF16)
    rest = x - hi.astype(F32)
    mid = rest.astype(BF16)
    return hi, mid, (rest - mid.astype(F32)).astype(BF16)


def spread_kernel(
    pitch_x, pitch_y, meta, anchors, select, triangles, arrived,
    posc, low, up, center, field, wyz, force,
):
    hosted = posc.shape[1]
    lanes = posc.shape[2]
    verts = arrived.shape[3]
    block_x = center.shape[1]

    field[...] = jnp.zeros_like(field)
    posc[0:3] = jnp.full((3, hosted, lanes), FAR, F32)
    for q in range(hosted):
        for a in range(3):
            posc[a, q : q + 1, 0:verts] = arrived[meta[0, q], a, pl.ds(meta[1, q], 1), :]
    for a in range(3):
        p = posc[a]
        turned = (0.5 * math.pi) * (p - 4.0 * jnp.floor(0.25 * p + 0.5))
        posc[3 + a] = jnp.cos(turned)
        posc[6 + a] = jnp.sin(turned)

    pos = posc[0:3]
    flat = pos.reshape(3 * hosted, lanes)
    parts = jnp.concatenate(split3(flat), axis=0)
    rows = 3 * hosted
    half_span = HALF - 3
    stiffness = 3.0 / half_span
    rest_sq = 2.0 * half_span * half_span
    ids = lax.broadcasted_iota(jnp.int32, (lanes, TRI_CHUNK), 0)

    def chunk(t, acc):
        at = pl.multiple_of(t * TRI_CHUNK, TRI_CHUNK)
        tables = [
            jnp.where(ids == triangles[k : k + 1, pl.ds(at, TRI_CHUNK)], 1.0, 0.0).astype(BF16)
            for k in range(3)
        ]
        table = jnp.concatenate(tables, axis=1)
        got = jnp.dot(parts, table, preferred_element_type=F32)
        got = got[0:rows] + got[rows : 2 * rows] + got[2 * rows : 3 * rows]
        corners = [got[:, TRI_CHUNK * k : TRI_CHUNK * (k + 1)] for k in range(3)]
        pushes = []
        for k in range(3):
            edge = corners[(k + 1) % 3] - corners[k]
            e = edge.reshape(3, hosted, TRI_CHUNK)
            stretch = stiffness * (jnp.sum(e * e, axis=0) / rest_sq - 1.0)
            pushes.append((stretch[None] * e).reshape(rows, TRI_CHUNK))
        net = jnp.concatenate([pushes[k] - pushes[(k + 2) % 3] for k in range(3)], axis=1)
        hi = net.astype(BF16)
        lo = (net - hi.astype(F32)).astype(BF16)
        return acc + lax.dot_general(
            jnp.concatenate([hi, lo], axis=0), table,
            (((1,), (1,)), ((), ())), preferred_element_type=F32,
        )

    chunks = triangles.shape[1] // TRI_CHUNK
    acc = lax.fori_loop(0, chunks, chunk, jnp.zeros((2 * rows, lanes), F32))
    force[...] = (acc[0:rows] + acc[rows:]).reshape(3, hosted, lanes)

    lane_ids = lax.broadcasted_iota(jnp.int32, (hosted, lanes), 1)
    square = lax.broadcasted_iota(jnp.int32, (hosted, hosted), 0) == lax.broadcasted_iota(
        jnp.int32, (hosted, hosted), 1
    )
    centres = []
    for a in range(3):
        mean = jnp.sum(jnp.where(lane_ids < verts, posc[a], 0.0), axis=1, keepdims=True) / verts
        column = anchors[a] + mean
        centres.append(jnp.sum(jnp.where(square, column, 0.0), axis=0, keepdims=True))
    for l in range(NB):
        offset = []
        for a in range(3):
            near = jnp.sum(jnp.where(select[l] > 0.5, centres[a], 0.0), axis=1, keepdims=True)
            offset.append((anchors[a] + posc[a]) - near)
        size_sq = offset[0] * offset[0] + offset[1] * offset[1] + offset[2] * offset[2]
        scale = repel_strength / (repel_radius_sq + size_sq)
        for a in range(3):
            force[a] += offset[a] * scale

    lane = lax.broadcasted_iota(jnp.int32, (BRICK, LANES), 1)

    def product(q, table):
        wx = cell_weights(posc, q, table)
        spread = jnp.concatenate(
            [force[a, pl.ds(q, 1), :] * wx for a in range(3)], axis=0
        ).astype(BF16)
        return lax.dot_general(
            spread, table[...], (((1,), (1,)), ((), ())), preferred_element_type=F32
        )

    def place(q, brick):
        z0 = meta[4, q]
        first = meta[2, q] * pitch_y + meta[3, q] + 4
        inside = (lane >= z0) & (lane < z0 + BRICK)
        for g in range(GROUPS):
            tile = brick[:, LANES * g : LANES * (g + 1)]
            for s in range(PER_TILE):
                turned = pltpu.roll(tile, lax.rem(z0 + LANES - SLOT * s, LANES), 1)
                for a in range(3):
                    here = pl.ds(
                        first + a * pitch_x * pitch_y + PER_TILE * g + s, BRICK, stride=pitch_y
                    )
                    field[here, :] += jnp.where(
                        inside, turned[BRICK * a : BRICK * (a + 1)], 0.0
                    )

    def step(t, carry):
        cells = [TOGETHER * t + i for i in range(TOGETHER)]
        bricks = [product(q, wyz.at[i]) for i, q in enumerate(cells)]
        for q, brick in zip(cells, bricks):
            place(q, brick)
        return carry

    lax.fori_loop(0, hosted // TOGETHER, step, 0)

    tall = low.shape[2]
    for a in range(3):

        def rim(x, carry):
            at = (a * pitch_x + x) * pitch_y
            low[a, x] = field[pl.ds(at, tall), :].astype(low.dtype)
            top = at + (HALF + block_x) * pitch_y
            up[a, x] = field[pl.ds(top, tall), :].astype(up.dtype)
            return carry

        def middle(x, carry):
            center[a, x] = field[pl.ds((a * pitch_x + HALF + x) * pitch_y, tall), :]
            return carry

        lax.fori_loop(0, HALF, rim, 0)
        lax.fori_loop(0, block_x, middle, 0)


def gather_kernel(
    pitch_x, pitch_y, meta, posc, own, col_low, col_up, row_low, row_up, out, lattice, wyz
):
    hosted = posc.shape[1]
    verts = out.shape[2]
    block_x, block_y = own.shape[1], own.shape[2]
    wide_y = row_low.shape[2]

    for a in range(3):

        def inner(x, carry):
            at = (a * pitch_x + HALF + x) * pitch_y
            lattice[pl.ds(at + HALF, block_y), :] = own[a, x].astype(F32)
            lattice[pl.ds(at, HALF), :] = col_low[a, x].astype(F32)
            lattice[pl.ds(at + HALF + block_y, HALF), :] = col_up[a, x].astype(F32)
            return carry

        def row_rim(x, carry):
            at = (a * pitch_x + x) * pitch_y
            lattice[pl.ds(at, wide_y), :] = row_low[a, x].astype(F32)
            top = at + (HALF + block_x) * pitch_y
            lattice[pl.ds(top, wide_y), :] = row_up[a, x].astype(F32)
            return carry

        lax.fori_loop(0, block_x, inner, 0)
        lax.fori_loop(0, HALF, row_rim, 0)

    slot_of = lax.broadcasted_iota(jnp.int32, (3 * BRICK, LANES), 1) // SLOT

    def cell(q, table):
        wx = cell_weights(posc, q, table)
        z0 = meta[4, q]
        first = meta[2, q] * pitch_y + meta[3, q]
        tiles = []
        for g in range(GROUPS):
            tile = None
            for s in range(PER_TILE):
                lines = jnp.concatenate(
                    [
                        lattice[
                            pl.ds(
                                first + a * pitch_x * pitch_y + PER_TILE * g + s,
                                BRICK,
                                stride=pitch_y,
                            ),
                            :,
                        ]
                        for a in range(3)
                    ],
                    axis=0,
                )
                turned = pltpu.roll(lines, lax.rem(LANES + SLOT * s - z0, LANES), 1)
                tile = turned if tile is None else jnp.where(slot_of == s, turned, tile)
            tiles.append(tile.astype(BF16))
        brick = jnp.concatenate(tiles, axis=1)
        projected = jnp.dot(brick, table[...], preferred_element_type=F32)
        found = jnp.sum(projected.reshape(3, BRICK, -1) * wx[None], axis=1)
        for a in range(3):
            out[a, pl.ds(q, 1), :] = found[a : a + 1, 0:verts]

    def step(t, carry):
        for i in range(TOGETHER):
            cell(TOGETHER * t + i, wyz.at[i])
        return carry

    lax.fori_loop(0, hosted // TOGETHER, step, 0)


def pack_kernel(table, out):
    capacity = out.shape[2]
    for d in range(out.shape[0]):
        for a in range(3):
            out[d, a] = table[a, capacity * d : capacity * (d + 1), :]


def fold_rims_kernel(center, up_in, low_in, left, right, stage_left, stage_right):
    block_x, tall = center.shape[1], center.shape[2]
    for a in range(3):

        def line(x, carry):
            for half, rim in ((0, up_in), (HALF, low_in)):
                first = center[a, half + x, 4 : 4 + HALF, :]
                last = center[a, half + x, tall - 16 : tall - 4, :]
                at = pl.ds((half + x) * HALF, HALF)
                stage_left[at, :] = first + rim[a, x, 0:16, :].astype(F32)[4:16]
                stage_right[at, :] = last + rim[a, x, tall - 16 :, :].astype(F32)[0:HALF]
            return carry

        lax.fori_loop(0, HALF, line, 0)
        left[a] = stage_left[...].astype(BF16)
        right[a] = stage_right[...].astype(BF16)


def total_kernel(after, center, up_in, low_in, right_in, left_in, out, stage_right, stage_left):
    block_y = out.shape[2]
    body = pl.ds(16, block_y)
    for a in range(3):
        stage_right[...] = right_in[a].astype(F32)
        stage_left[...] = left_in[a].astype(F32)

        def line(x, carry):
            for half, rim in ((0, up_in), (HALF, low_in)):
                at = pl.ds((half + x) * HALF, HALF)
                out[a, half + x] = center[a, half + x, body, :] + rim[a, x, body, :].astype(F32)
                out[a, half + x, 0:HALF, :] += stage_right[at, :]
                out[a, half + x, block_y - HALF :, :] += stage_left[at, :]
            return carry

        lax.fori_loop(0, HALF, line, 0)


def on_device(velocity, host_owner, host_site, vertices, triangles, neighbours):
    columns = lax.axis_size("col")
    rows = lax.axis_size("row")
    capacity = vertices.shape[0] // columns
    verts = vertices.shape[2]
    lanes = padded_to(verts, LANES)
    hosted = host_owner.shape[0]
    block_x, block_y, depth = velocity.shape[1:]
    wide_x, wide_y = block_x + 2 * HALF, block_y + 2 * HALF
    smem = pl.BlockSpec(memory_space=pltpu.SMEM)
    vmem = pl.BlockSpec(memory_space=pltpu.VMEM)
    params = pltpu.CompilerParams(vmem_limit_bytes=VMEM_LIMIT)

    packed = pl.pallas_call(
        pack_kernel,
        out_shape=jax.ShapeDtypeStruct((columns, 3, capacity, verts), F32),
        in_specs=[vmem],
        out_specs=vmem,
        compiler_params=params,
        cost_estimate=pl.CostEstimate(
            flops=20_000_000_000, bytes_accessed=60_000_000, transcendentals=0
        ),
        name="pack_vertices",
    )(vertices.transpose(1, 0, 2))
    head, tail = velocity[:, :, 0:HALF], velocity[:, :, block_y - HALF :]
    col_low = from_previous(tail, "col", columns - 1, columns)
    col_up = from_next(head, "col", columns - 1, columns)
    arrived = lax.all_to_all(packed, "col", split_axis=0, concat_axis=0, tiled=True)

    owners = host_owner[:, 0]
    ids = jnp.arange(hosted, dtype=jnp.int32)
    earlier = ids[None, :] < ids[:, None]
    ranking = jnp.sum(
        ((owners[:, None] == owners[None, :]) & earlier).astype(jnp.int32), axis=1
    )
    meta = jnp.stack([owners, ranking, host_site[0], host_site[1], host_site[2] - HALF])
    origin = jnp.stack(
        [lax.axis_index("row") * block_x, lax.axis_index("col") * block_y, jnp.int32(0)]
    ).astype(jnp.int32)
    anchors = (host_site + origin[:, None]).astype(F32)[:, :, None]
    select = (neighbours[:, :, None] == ids[None, None, :]).astype(F32)

    tall = block_y + 2 * (HALF + 4)
    field_pitch = tall + 1
    posc, low, up, center = pl.pallas_call(
        functools.partial(spread_kernel, wide_x, field_pitch),
        out_shape=(
            jax.ShapeDtypeStruct((9, hosted, lanes), F32),
            jax.ShapeDtypeStruct((3, HALF, tall, depth), BF16),
            jax.ShapeDtypeStruct((3, HALF, tall, depth), BF16),
            jax.ShapeDtypeStruct((3, block_x, tall, depth), F32),
        ),
        in_specs=[smem] + [vmem] * 4,
        out_specs=(vmem, vmem, vmem, vmem),
        scratch_shapes=[
            pltpu.VMEM((3 * wide_x * field_pitch, depth), F32),
            pltpu.VMEM((TOGETHER, SLOT * BRICK, lanes), BF16),
            pltpu.VMEM((3, hosted, lanes), F32),
        ],
        compiler_params=params,
        cost_estimate=pl.CostEstimate(
            flops=20_000_000_000, bytes_accessed=60_000_000, transcendentals=0
        ),
        name="spread_forces",
    )(meta, anchors, select, triangles, arrived)

    up, low, col_low, col_up = lax.optimization_barrier((up, low, col_low, col_up))
    up_in = from_previous(up, "row", rows - 1, rows)
    low_in = from_next(low, "row", rows - 1, rows)

    strip = jax.ShapeDtypeStruct((3, block_x * HALF, depth), BF16)
    stage = pltpu.VMEM((block_x * HALF, depth), F32)
    left, right = pl.pallas_call(
        fold_rims_kernel,
        out_shape=(strip, strip),
        in_specs=[vmem] * 3,
        out_specs=(vmem, vmem),
        scratch_shapes=[stage, stage],
        compiler_params=params,
        name="fold_rims",
    )(center, up_in, low_in)
    right_in = from_previous(right, "col", columns - 1, columns)
    left_in = from_next(left, "col", columns - 1, columns)
    widened = jnp.concatenate([col_low, velocity, col_up], axis=2)
    head, tail = widened[:, 0:HALF], widened[:, block_x - HALF :]
    row_low = from_previous(tail, "row", rows - 1, rows)
    row_up = from_next(head, "row", rows - 1, rows)

    lattice_pitch = padded_to(wide_y, 8) + 1
    velocities = pl.pallas_call(
        functools.partial(gather_kernel, wide_x, lattice_pitch),
        out_shape=jax.ShapeDtypeStruct((3, hosted, verts), F32),
        in_specs=[smem, vmem, vmem, vmem, vmem, vmem, vmem],
        out_specs=vmem,
        scratch_shapes=[
            pltpu.VMEM((3 * wide_x * lattice_pitch, depth), F32),
            pltpu.VMEM((TOGETHER, SLOT * BRICK, lanes), BF16),
        ],
        compiler_params=params,
        cost_estimate=pl.CostEstimate(
            flops=10_000_000_000, bytes_accessed=30_000_000, transcendentals=0
        ),
        name="interpolate_velocity",
    )(meta, posc, velocity, col_low, col_up, row_low, row_up)

    force_field = pl.pallas_call(
        total_kernel,
        out_shape=jax.ShapeDtypeStruct((3, block_x, block_y, depth), F32),
        in_specs=[pl.BlockSpec(memory_space=pl.ANY)] + [vmem] * 5,
        out_specs=vmem,
        scratch_shapes=[stage, stage],
        compiler_params=params,
        name="total_force",
    )(velocities, center, up_in, low_in, right_in, left_in)
    return (force_field, velocities.transpose(1, 0, 2))


def solution(mesh):
    return jax.shard_map(
        on_device,
        mesh=mesh,
        in_specs=(
            P(None, "row", "col", None),
            P(("row", "col"), None),
            P(None, ("row", "col")),
            P(("row", "col"), None, None),
            P(),
            P(None, ("row", "col")),
        ),
        out_specs=(P(None, "row", "col", None), P(("row", "col"), None, None)),
        check_vma=False,
    )
```

```python
import functools
import math

import jax
import jax.numpy as jnp
from jax import lax
from jax.experimental import pallas as pl
from jax.experimental.pallas import tpu as pltpu
from jax.sharding import PartitionSpec as P

BRICK = 24
HALF = 12
REACH = 10
TALL = 56
EDGE = HALF - REACH
NB = 4
LANES = 128
SLOT = 32
PER_TILE = LANES // SLOT
GROUPS = BRICK // PER_TILE
TRI_CHUNK = 256
TOGETHER = 4
FAR = 64.0

repel_strength = 160.0
repel_radius_sq = 64.0

F32 = jnp.float32
BF16 = jnp.bfloat16
VMEM_LIMIT = 24 * 1024 * 1024


def padded_to(size, multiple):
    return -(-size // multiple) * multiple


def exchange(even, odd, axis):
    count = lax.axis_size(axis)
    pairs = [(i, i + 1) for i in range(1, count - 1, 2)]
    return (
        lax.ppermute(even, axis, [(i, i ^ 1) for i in range(count)]),
        lax.ppermute(odd, axis, pairs + [(j, i) for i, j in pairs]),
    )


def outgoing(stage, odd, even_out, odd_out, a):
    for parity in range(2):

        @pl.when(odd == parity)
        def _():
            even_out[a] = stage[1 - parity][...].astype(BF16)
            odd_out[a] = stage[parity][...].astype(BF16)


def incoming(stage, odd, even_in, odd_in, a):
    for parity in range(2):

        @pl.when(odd == parity)
        def _():
            stage[1 - parity][...] = even_in[a].astype(F32)
            stage[parity][...] = odd_in[a].astype(F32)


def node_weights(p, c, s, rows):
    lanes = p.shape[1]
    r = lax.broadcasted_iota(jnp.int32, (8, lanes), 0)
    base = jnp.where(r % 2 == 1, s, c)
    pattern = 0.25 * (1.0 + jnp.where(r % 4 >= 2, -base, base))
    nodes = (r - HALF).astype(F32)
    parts = []
    for block in range(rows // 8):
        distance = p - (nodes + 8.0 * block)
        parts.append(jnp.where(jnp.abs(distance) < 2.0, pattern, 0.0))
    return jnp.concatenate(parts, axis=0)


def cell_weights(posc, q, wyz):
    row = lambda kind: posc[kind, pl.ds(q, 1), :]
    wx, wy, wz = (node_weights(row(a), row(3 + a), row(6 + a), BRICK) for a in range(3))
    empty = jnp.zeros((SLOT - BRICK, wz.shape[1]), F32)
    for j in range(BRICK):
        wyz[SLOT * j : SLOT * (j + 1), :] = jnp.concatenate(
            [wy[j : j + 1] * wz, empty], axis=0
        ).astype(BF16)
    return wx


def split3(x):
    hi = x.astype(BF16)
    rest = x - hi.astype(F32)
    mid = rest.astype(BF16)
    return hi, mid, (rest - mid.astype(F32)).astype(BF16)


def spread_kernel(
    pitch_x, pitch_y, spot, site, columns, triangles, arrived,
    posc, row_even, row_odd, center, field, wyz, force, *stage,
):
    hosted = posc.shape[1]
    lanes = posc.shape[2]
    verts = arrived.shape[3]
    block_x = center.shape[1]

    field[...] = jnp.zeros_like(field)
    posc[0:3] = jnp.full((3, hosted, lanes), FAR, F32)
    for q in range(hosted):
        rank = 0
        for p in range(q):
            rank = rank + (site[3, p] == site[3, q]).astype(jnp.int32)
        for a in range(3):
            posc[a, q : q + 1, 0:verts] = arrived[site[3, q], a, pl.ds(rank, 1), :]
    for a in range(3):
        p = posc[a]
        turned = (0.5 * math.pi) * (p - 4.0 * jnp.floor(0.25 * p + 0.5))
        posc[3 + a] = jnp.cos(turned)
        posc[6 + a] = jnp.sin(turned)

    pos = posc[0:3]
    flat = pos.reshape(3 * hosted, lanes)
    parts = jnp.concatenate(split3(flat), axis=0)
    rows = 3 * hosted
    half_span = HALF - 3
    stiffness = 3.0 / half_span
    rest_sq = 2.0 * half_span * half_span
    ids = lax.broadcasted_iota(jnp.int32, (lanes, TRI_CHUNK), 0)

    def chunk(t, acc):
        at = pl.multiple_of(t * TRI_CHUNK, TRI_CHUNK)
        tables = [
            jnp.where(ids == triangles[k : k + 1, pl.ds(at, TRI_CHUNK)], 1.0, 0.0).astype(BF16)
            for k in range(3)
        ]
        table = jnp.concatenate(tables, axis=1)
        got = jnp.dot(parts, table, preferred_element_type=F32)
        got = got[0:rows] + got[rows : 2 * rows] + got[2 * rows : 3 * rows]
        corners = [got[:, TRI_CHUNK * k : TRI_CHUNK * (k + 1)] for k in range(3)]
        pushes = []
        for k in range(3):
            edge = corners[(k + 1) % 3] - corners[k]
            e = edge.reshape(3, hosted, TRI_CHUNK)
            stretch = stiffness * (jnp.sum(e * e, axis=0) / rest_sq - 1.0)
            pushes.append((stretch[None] * e).reshape(rows, TRI_CHUNK))
        net = jnp.concatenate([pushes[k] - pushes[(k + 2) % 3] for k in range(3)], axis=1)
        hi = net.astype(BF16)
        lo = (net - hi.astype(F32)).astype(BF16)
        return acc + lax.dot_general(
            jnp.concatenate([hi, lo], axis=0), table,
            (((1,), (1,)), ((), ())), preferred_element_type=F32,
        )

    chunks = triangles.shape[1] // TRI_CHUNK
    acc = lax.fori_loop(0, chunks, chunk, jnp.zeros((2 * rows, lanes), F32))
    force[...] = (acc[0:rows] + acc[rows:]).reshape(3, hosted, lanes)

    lane_ids = lax.broadcasted_iota(jnp.int32, (hosted, lanes), 1)
    across = lax.broadcasted_iota(jnp.int32, (hosted, hosted), 1)
    square = lax.broadcasted_iota(jnp.int32, (hosted, hosted), 0) == across
    anchors = [(columns[:, a : a + 1] + spot[a]).astype(F32) for a in range(3)]
    centres = []
    for a in range(3):
        mean = jnp.sum(jnp.where(lane_ids < verts, posc[a], 0.0), axis=1, keepdims=True) / verts
        column = anchors[a] + mean
        centres.append(jnp.sum(jnp.where(square, column, 0.0), axis=0, keepdims=True))
    for l in range(NB):
        offset = []
        for a in range(3):
            near = jnp.sum(jnp.where(columns[:, 3 + l : 4 + l] == across, centres[a], 0.0), axis=1, keepdims=True)
            offset.append((anchors[a] + posc[a]) - near)
        size_sq = offset[0] * offset[0] + offset[1] * offset[1] + offset[2] * offset[2]
        scale = repel_strength / (repel_radius_sq + size_sq)
        for a in range(3):
            force[a] += offset[a] * scale

    lane = lax.broadcasted_iota(jnp.int32, (BRICK, LANES), 1)

    def product(q, table):
        wx = cell_weights(posc, q, table)
        spread = jnp.concatenate(
            [force[a, pl.ds(q, 1), :] * wx for a in range(3)], axis=0
        ).astype(BF16)
        return lax.dot_general(
            spread, table[...], (((1,), (1,)), ((), ())), preferred_element_type=F32
        )

    def place(q, brick):
        z0 = site[2, q] - HALF
        first = site[0, q] * pitch_y + site[1, q] + 4
        inside = (lane >= z0) & (lane < z0 + BRICK)
        for g in range(GROUPS):
            tile = brick[:, LANES * g : LANES * (g + 1)]
            for s in range(PER_TILE):
                turned = pltpu.roll(tile, lax.rem(z0 + LANES - SLOT * s, LANES), 1)
                for a in range(3):
                    here = pl.ds(
                        first + a * pitch_x * pitch_y + PER_TILE * g + s, BRICK, stride=pitch_y
                    )
                    field[here, :] += jnp.where(
                        inside, turned[BRICK * a : BRICK * (a + 1)], 0.0
                    )

    def step(t, carry):
        cells = [TOGETHER * t + i for i in range(TOGETHER)]
        bricks = [product(q, wyz.at[i]) for i, q in enumerate(cells)]
        for q, brick in zip(cells, bricks):
            place(q, brick)
        return carry

    lax.fori_loop(0, hosted // TOGETHER, step, 0)

    tall = center.shape[2]
    for a in range(3):

        def rim(x, carry):
            at = (a * pitch_x + EDGE + x) * pitch_y + 4
            to = pl.ds(pl.multiple_of(x * TALL, 8), TALL)
            stage[0][to, :] = field[pl.ds(at, TALL), :]
            stage[1][to, :] = field[pl.ds(at + (REACH + block_x) * pitch_y, TALL), :]
            return carry

        def middle(x, carry):
            center[a, x] = field[pl.ds((a * pitch_x + HALF + x) * pitch_y, tall), :]
            return carry

        lax.fori_loop(0, REACH, rim, 0, unroll=5)
        lax.fori_loop(0, block_x, middle, 0, unroll=4)
        outgoing(stage, spot[3], row_even, row_odd, a)


def gather_kernel(
    pitch_x, pitch_y, spot, site, posc, own, col_even, col_odd, row_even, row_odd, out, token,
    lattice, wyz, *stages,
):
    col_stage, row_stage = stages[:2], stages[2:]
    hosted = posc.shape[1]
    verts = out.shape[2]
    block_x, block_y = own.shape[1], own.shape[2]
    blank = jnp.zeros((TALL, lattice.shape[1]), F32)

    for a in range(3):
        incoming(col_stage, spot[4], col_even, col_odd, a)
        incoming(row_stage, spot[3], row_even, row_odd, a)

        def inner(x, carry):
            at = (a * pitch_x + HALF + x) * pitch_y
            rim = pl.ds(x * REACH, REACH)
            lattice[pl.ds(at, EDGE), :] = blank[0:EDGE]
            lattice[pl.ds(at + EDGE, REACH), :] = col_stage[0][rim, :]
            lattice[pl.ds(at + HALF, block_y), :] = own[a, x].astype(F32)
            lattice[pl.ds(at + HALF + block_y, REACH), :] = col_stage[1][rim, :]
            lattice[pl.ds(at + HALF + block_y + REACH, EDGE), :] = blank[0:EDGE]
            return carry

        def row_rim(x, carry):
            at = (a * pitch_x + EDGE + x) * pitch_y
            line = pl.ds(pl.multiple_of(x * TALL, 8), TALL)
            lattice[pl.ds(at, TALL), :] = row_stage[0][line, :]
            top = at + (REACH + block_x) * pitch_y
            lattice[pl.ds(top, TALL), :] = row_stage[1][line, :]
            return carry

        lax.fori_loop(0, block_x, inner, 0, unroll=4)
        lax.fori_loop(0, REACH, row_rim, 0, unroll=5)
        for x in (*range(EDGE), *range(pitch_x - EDGE, pitch_x)):
            lattice[pl.ds((a * pitch_x + x) * pitch_y, TALL), :] = blank

    token[...] = jnp.zeros_like(token)
    slot_of = lax.broadcasted_iota(jnp.int32, (3 * BRICK, LANES), 1) // SLOT

    def cell(q, table):
        wx = cell_weights(posc, q, table)
        z0 = site[2, q] - HALF
        first = site[0, q] * pitch_y + site[1, q]
        tiles = []
        for g in range(GROUPS):
            tile = None
            for s in range(PER_TILE):
                lines = jnp.concatenate(
                    [
                        lattice[
                            pl.ds(
                                first + a * pitch_x * pitch_y + PER_TILE * g + s,
                                BRICK,
                                stride=pitch_y,
                            ),
                            :,
                        ]
                        for a in range(3)
                    ],
                    axis=0,
                )
                turned = pltpu.roll(lines, lax.rem(LANES + SLOT * s - z0, LANES), 1)
                tile = turned if tile is None else jnp.where(slot_of == s, turned, tile)
            tiles.append(tile.astype(BF16))
        brick = jnp.concatenate(tiles, axis=1)
        projected = jnp.dot(brick, table[...], preferred_element_type=F32)
        found = jnp.sum(projected.reshape(3, BRICK, -1) * wx[None], axis=1)
        for a in range(3):
            out[a, pl.ds(q, 1), :] = found[a : a + 1, 0:verts]

    def step(t, carry):
        for i in range(TOGETHER):
            cell(TOGETHER * t + i, wyz.at[i])
        return carry

    lax.fori_loop(0, hosted // TOGETHER, step, 0)


def pack_kernel(spot, table, own, out, col_even, col_odd, *stage):
    capacity = out.shape[2]
    block_x, block_y = own.shape[1], own.shape[2]
    for d in range(out.shape[0]):
        for a in range(3):
            out[d, a] = table[a, capacity * d : capacity * (d + 1), :]
    for a in range(3):

        def line(x, carry):
            cells = own[a, x].astype(F32)
            to = pl.ds(x * REACH, REACH)
            stage[0][to, :] = cells[0:REACH]
            stage[1][to, :] = cells[block_y - REACH :]
            return carry

        lax.fori_loop(0, block_x, line, 0, unroll=4)
        outgoing(stage, spot[4], col_even, col_odd, a)


def widen_kernel(spot, own, col_even, col_odd, row_even, row_odd, *stages):
    block_x, block_y = own.shape[1], own.shape[2]
    col_stage, wide = stages[:2], stages[2:]
    for ref in wide:
        ref[...] = jnp.zeros_like(ref)
    for a in range(3):
        incoming(col_stage, spot[4], col_even, col_odd, a)
        for side, first in enumerate((0, block_x - REACH)):

            def line(x, carry):
                at = x * TALL + HALF
                rim = pl.ds((first + x) * REACH, REACH)
                wide[side][pl.ds(at - REACH, REACH), :] = col_stage[0][rim, :]
                wide[side][pl.ds(at, block_y), :] = own[a, first + x].astype(F32)
                wide[side][pl.ds(at + block_y, REACH), :] = col_stage[1][rim, :]
                return carry

            lax.fori_loop(0, REACH, line, 0, unroll=5)
        outgoing(wide, spot[3], row_even, row_odd, a)


def fill_rims(rim, odd, even_in, odd_in, a):
    reached = REACH * TALL
    far = rim.shape[0] - reached
    rim[reached:far, :] = jnp.zeros((far - reached, rim.shape[1]), F32)
    for parity in range(2):

        @pl.when(odd == parity)
        def _():
            rim[(1 - parity) * far : (1 - parity) * far + reached, :] = even_in[a].astype(F32)
            rim[parity * far : parity * far + reached, :] = odd_in[a].astype(F32)


def fold_rims_kernel(spot, center, row_even, row_odd, col_even, col_odd, rim, *stage):
    block_x, tall = center.shape[1], center.shape[2]
    for a in range(3):
        fill_rims(rim, spot[3], row_even, row_odd, a)

        def line(x, carry):
            at = x * TALL
            to = pl.ds(x * REACH, REACH)
            low, high = EDGE, TALL - HALF
            for side, y in enumerate((low, high)):
                stage[side][to, :] = (
                    center[a, x, y + 4 : y + 4 + REACH, :] + rim[pl.ds(at + y, REACH), :]
                )
            return carry

        lax.fori_loop(0, block_x, line, 0, unroll=4)
        outgoing(stage, spot[4], col_even, col_odd, a)


def total_kernel(
    after, spot, center, row_even, row_odd, col_even, col_odd, out, rim, *stage
):
    block_x, block_y = out.shape[1], out.shape[2]
    for a in range(3):
        fill_rims(rim, spot[3], row_even, row_odd, a)
        incoming(stage, spot[4], col_even, col_odd, a)

        def line(x, carry):
            at = pl.ds(x * REACH, REACH)
            body = rim[pl.ds(x * TALL + HALF, block_y), :]
            out[a, x] = center[a, x, pl.ds(HALF + 4, block_y), :] + body
            out[a, x, 0:REACH, :] += stage[0][at, :]
            out[a, x, block_y - REACH :, :] += stage[1][at, :]
            return carry

        lax.fori_loop(0, block_x, line, 0, unroll=4)


def on_device(velocity, host_owner, host_site, vertices, triangles, neighbours):
    columns = lax.axis_size("col")
    capacity = vertices.shape[0] // columns
    verts = vertices.shape[2]
    lanes = padded_to(verts, LANES)
    hosted = host_owner.shape[0]
    block_x, block_y, depth = velocity.shape[1:]
    wide_x, wide_y = block_x + 2 * HALF, block_y + 2 * HALF
    smem = pl.BlockSpec(memory_space=pltpu.SMEM)
    vmem = pl.BlockSpec(memory_space=pltpu.VMEM)
    params = pltpu.CompilerParams(vmem_limit_bytes=VMEM_LIMIT)
    strip = jax.ShapeDtypeStruct((3, block_x * REACH, depth), BF16)
    stage = [pltpu.VMEM((block_x * REACH, depth), F32)] * 2
    long_strip = jax.ShapeDtypeStruct((3, REACH * TALL, depth), BF16)
    long_stage = [pltpu.VMEM((REACH * TALL, depth), F32)] * 2
    rim_stage = pltpu.VMEM((block_x * TALL, depth), F32)

    row, col = lax.axis_index("row"), lax.axis_index("col")
    spot = jnp.stack([row * block_x, col * block_y, 0 * row, row & 1, col & 1]).astype(jnp.int32)
    places = jnp.concatenate([host_site, host_owner.T], axis=0)
    listed = jnp.concatenate([host_site, neighbours], axis=0).T

    packed, col_even, col_odd = pl.pallas_call(
        pack_kernel,
        out_shape=(jax.ShapeDtypeStruct((columns, 3, capacity, verts), F32), strip, strip),
        in_specs=[smem, vmem, vmem],
        out_specs=(vmem,) * 3,
        scratch_shapes=stage,
        compiler_params=params,
        name="pack_vertices",
    )(spot, vertices.transpose(1, 0, 2), velocity)
    near_even, near_odd = exchange(col_even, col_odd, "col")
    arrived = lax.all_to_all(packed, "col", split_axis=0, concat_axis=0, tiled=True)

    tall = block_y + 2 * (HALF + 4)
    field_pitch = tall + 1
    posc, row_even, row_odd, center = pl.pallas_call(
        functools.partial(spread_kernel, wide_x, field_pitch),
        out_shape=(
            jax.ShapeDtypeStruct((9, hosted, lanes), F32),
            long_strip,
            long_strip,
            jax.ShapeDtypeStruct((3, block_x, tall, depth), F32),
        ),
        in_specs=[smem, smem, vmem, vmem, vmem],
        out_specs=(vmem,) * 4,
        scratch_shapes=[
            pltpu.VMEM((3 * wide_x * field_pitch, depth), F32),
            pltpu.VMEM((TOGETHER, SLOT * BRICK, lanes), BF16),
            pltpu.VMEM((3, hosted, lanes), F32),
            *long_stage,
        ],
        compiler_params=params,
        cost_estimate=pl.CostEstimate(
            flops=20_000_000_000, bytes_accessed=60_000_000, transcendentals=0
        ),
        name="spread_forces",
    )(spot, places, listed, triangles, arrived)

    row_even, row_odd, near_even, near_odd = lax.optimization_barrier(
        (row_even, row_odd, near_even, near_odd)
    )
    row_even, row_odd = exchange(row_even, row_odd, "row")
    col_even, col_odd = pl.pallas_call(
        fold_rims_kernel,
        out_shape=(strip, strip),
        in_specs=[smem, vmem, vmem, vmem],
        out_specs=(vmem, vmem),
        scratch_shapes=[rim_stage, *stage],
        compiler_params=params,
        name="fold_rims",
    )(spot, center, row_even, row_odd)
    col_even, col_odd = exchange(col_even, col_odd, "col")

    wide_even, wide_odd = pl.pallas_call(
        widen_kernel,
        out_shape=(long_strip, long_strip),
        in_specs=[smem, vmem, vmem, vmem],
        out_specs=(vmem, vmem),
        scratch_shapes=stage + long_stage,
        compiler_params=params,
        name="widen_rims",
    )(spot, velocity, near_even, near_odd)
    wide_even, wide_odd = exchange(wide_even, wide_odd, "row")

    lattice_pitch = padded_to(wide_y, 8) + 1
    velocities, token = pl.pallas_call(
        functools.partial(gather_kernel, wide_x, lattice_pitch),
        out_shape=(
            jax.ShapeDtypeStruct((3, hosted, verts), F32),
            jax.ShapeDtypeStruct((8, LANES), F32),
        ),
        in_specs=[smem, smem] + [vmem] * 6,
        out_specs=(vmem, vmem),
        scratch_shapes=[
            pltpu.VMEM((3 * wide_x * lattice_pitch, depth), F32),
            pltpu.VMEM((TOGETHER, SLOT * BRICK, lanes), BF16),
            *stage,
            *long_stage,
        ],
        compiler_params=params,
        cost_estimate=pl.CostEstimate(
            flops=10_000_000_000, bytes_accessed=30_000_000, transcendentals=0
        ),
        name="interpolate_velocity",
    )(spot, places, posc, velocity, near_even, near_odd, wide_even, wide_odd)

    force_field = pl.pallas_call(
        total_kernel,
        out_shape=jax.ShapeDtypeStruct((3, block_x, block_y, depth), F32),
        in_specs=[vmem, smem] + [vmem] * 5,
        out_specs=vmem,
        scratch_shapes=[rim_stage, *stage],
        compiler_params=params,
        name="total_force",
    )(token, spot, center, row_even, row_odd, col_even, col_odd)
    return (force_field, velocities.transpose(1, 0, 2))


def solution(mesh):
    return jax.shard_map(
        on_device,
        mesh=mesh,
        in_specs=(
            P(None, "row", "col", None),
            P(("row", "col"), None),
            P(None, ("row", "col")),
            P(("row", "col"), None, None),
            P(),
            P(None, ("row", "col")),
        ),
        out_specs=(P(None, "row", "col", None), P(("row", "col"), None, None)),
        check_vma=False,
    )
```

```python
import functools
import math

import jax
import jax.numpy as jnp
from jax import lax
from jax.experimental import pallas as pl
from jax.experimental.pallas import tpu as pltpu
from jax.sharding import PartitionSpec as P

BRICK = 24
HALF = 12
REACH = 10
TALL = 56
EDGE = HALF - REACH
NB = 4
LANES = 128
SLOT = 32
PER_TILE = LANES // SLOT
GROUPS = BRICK // PER_TILE
TRI_CHUNK = 256
TOGETHER = 4
FAR = 64.0

repel_strength = 160.0
repel_radius_sq = 64.0

F32 = jnp.float32
BF16 = jnp.bfloat16
VMEM_LIMIT = 24 * 1024 * 1024


def padded_to(size, multiple):
    return -(-size // multiple) * multiple


def exchange(even, odd, axis):
    count = lax.axis_size(axis)
    pairs = [(i, i + 1) for i in range(1, count - 1, 2)]
    return (
        lax.ppermute(even, axis, [(i, i ^ 1) for i in range(count)]),
        lax.ppermute(odd, axis, pairs + [(j, i) for i, j in pairs]),
    )


def outgoing(stage, odd, even_out, odd_out, a):
    for parity in range(2):

        @pl.when(odd == parity)
        def _():
            even_out[a] = stage[1 - parity][...].astype(BF16)
            odd_out[a] = stage[parity][...].astype(BF16)


def incoming(stage, odd, even_in, odd_in, a):
    for parity in range(2):

        @pl.when(odd == parity)
        def _():
            stage[1 - parity][...] = even_in[a].astype(F32)
            stage[parity][...] = odd_in[a].astype(F32)


def node_weights(p, c, s, rows):
    lanes = p.shape[1]
    r = lax.broadcasted_iota(jnp.int32, (8, lanes), 0)
    base = jnp.where(r % 2 == 1, s, c)
    pattern = 0.25 * (1.0 + jnp.where(r % 4 >= 2, -base, base))
    nodes = (r - HALF).astype(F32)
    parts = []
    for block in range(rows // 8):
        distance = p - (nodes + 8.0 * block)
        parts.append(jnp.where(jnp.abs(distance) < 2.0, pattern, 0.0))
    return jnp.concatenate(parts, axis=0)


def cell_weights(posc, q, wyz):
    row = lambda kind: posc[kind, pl.ds(q, 1), :]
    wx, wy, wz = (node_weights(row(a), row(3 + a), row(6 + a), BRICK) for a in range(3))
    empty = jnp.zeros((SLOT - BRICK, wz.shape[1]), F32)
    for j in range(BRICK):
        wyz[SLOT * j : SLOT * (j + 1), :] = jnp.concatenate(
            [wy[j : j + 1] * wz, empty], axis=0
        ).astype(BF16)
    return wx


def split3(x):
    hi = x.astype(BF16)
    rest = x - hi.astype(F32)
    mid = rest.astype(BF16)
    return hi, mid, (rest - mid.astype(F32)).astype(BF16)


def spread_kernel(
    pitch_x, pitch_y, spot, site, columns, triangles, arrived,
    posc, row_even, row_odd, center, field, wyz, force, *stage,
):
    hosted = posc.shape[1]
    lanes = posc.shape[2]
    verts = arrived.shape[3]
    block_x = center.shape[1]

    field[...] = jnp.zeros_like(field)
    posc[0:3] = jnp.full((3, hosted, lanes), FAR, F32)
    for q in range(hosted):
        rank = 0
        for p in range(q):
            rank = rank + (site[3, p] == site[3, q]).astype(jnp.int32)
        for a in range(3):
            posc[a, q : q + 1, 0:verts] = arrived[site[3, q], a, pl.ds(rank, 1), :]
    for a in range(3):
        p = posc[a]
        turned = (0.5 * math.pi) * (p - 4.0 * jnp.floor(0.25 * p + 0.5))
        posc[3 + a] = jnp.cos(turned)
        posc[6 + a] = jnp.sin(turned)

    pos = posc[0:3]
    flat = pos.reshape(3 * hosted, lanes)
    parts = jnp.concatenate(split3(flat), axis=0)
    rows = 3 * hosted
    half_span = HALF - 3
    stiffness = 3.0 / half_span
    rest_sq = 2.0 * half_span * half_span
    ids = lax.broadcasted_iota(jnp.int32, (lanes, TRI_CHUNK), 0)

    def chunk(t, acc):
        at = pl.multiple_of(t * TRI_CHUNK, TRI_CHUNK)
        tables = [
            jnp.where(ids == triangles[k : k + 1, pl.ds(at, TRI_CHUNK)], 1.0, 0.0).astype(BF16)
            for k in range(3)
        ]
        table = jnp.concatenate(tables, axis=1)
        got = jnp.dot(parts, table, preferred_element_type=F32)
        got = got[0:rows] + got[rows : 2 * rows] + got[2 * rows : 3 * rows]
        corners = [got[:, TRI_CHUNK * k : TRI_CHUNK * (k + 1)] for k in range(3)]
        pushes = []
        for k in range(3):
            edge = corners[(k + 1) % 3] - corners[k]
            e = edge.reshape(3, hosted, TRI_CHUNK)
            stretch = stiffness * (jnp.sum(e * e, axis=0) / rest_sq - 1.0)
            pushes.append((stretch[None] * e).reshape(rows, TRI_CHUNK))
        net = jnp.concatenate([pushes[k] - pushes[(k + 2) % 3] for k in range(3)], axis=1)
        hi = net.astype(BF16)
        lo = (net - hi.astype(F32)).astype(BF16)
        return acc + lax.dot_general(
            jnp.concatenate([hi, lo], axis=0), table,
            (((1,), (1,)), ((), ())), preferred_element_type=F32,
        )

    chunks = triangles.shape[1] // TRI_CHUNK
    acc = lax.fori_loop(0, chunks, chunk, jnp.zeros((2 * rows, lanes), F32), unroll=True)
    force[...] = (acc[0:rows] + acc[rows:]).reshape(3, hosted, lanes)

    lane_ids = lax.broadcasted_iota(jnp.int32, (hosted, lanes), 1)
    across = lax.broadcasted_iota(jnp.int32, (hosted, hosted), 1)
    square = lax.broadcasted_iota(jnp.int32, (hosted, hosted), 0) == across
    anchors = [(columns[:, a : a + 1] + spot[a]).astype(F32) for a in range(3)]
    centres = []
    for a in range(3):
        mean = jnp.sum(jnp.where(lane_ids < verts, posc[a], 0.0), axis=1, keepdims=True) / verts
        column = anchors[a] + mean
        centres.append(jnp.sum(jnp.where(square, column, 0.0), axis=0, keepdims=True))
    for l in range(NB):
        offset = []
        for a in range(3):
            near = jnp.sum(jnp.where(columns[:, 3 + l : 4 + l] == across, centres[a], 0.0), axis=1, keepdims=True)
            offset.append((anchors[a] + posc[a]) - near)
        size_sq = offset[0] * offset[0] + offset[1] * offset[1] + offset[2] * offset[2]
        scale = repel_strength / (repel_radius_sq + size_sq)
        for a in range(3):
            force[a] += offset[a] * scale

    lane = lax.broadcasted_iota(jnp.int32, (BRICK, LANES), 1)

    def product(q, table):
        wx = cell_weights(posc, q, table)
        spread = jnp.concatenate(
            [force[a, pl.ds(q, 1), :] * wx for a in range(3)], axis=0
        ).astype(BF16)
        return lax.dot_general(
            spread, table[...], (((1,), (1,)), ((), ())), preferred_element_type=F32
        )

    def place(q, brick):
        z0 = site[2, q] - HALF
        first = site[0, q] * pitch_y + site[1, q] + 4
        inside = (lane >= z0) & (lane < z0 + BRICK)
        for g in range(GROUPS):
            tile = brick[:, LANES * g : LANES * (g + 1)]
            for s in range(PER_TILE):
                turned = pltpu.roll(tile, lax.rem(z0 + LANES - SLOT * s, LANES), 1)
                for a in range(3):
                    here = pl.ds(
                        first + a * pitch_x * pitch_y + PER_TILE * g + s, BRICK, stride=pitch_y
                    )
                    field[here, :] += jnp.where(
                        inside, turned[BRICK * a : BRICK * (a + 1)], 0.0
                    )

    def step(t, carry):
        cells = [TOGETHER * t + i for i in range(TOGETHER)]
        bricks = [product(q, wyz.at[i]) for i, q in enumerate(cells)]
        for q, brick in zip(cells, bricks):
            place(q, brick)
        return carry

    lax.fori_loop(0, hosted // TOGETHER, step, 0)

    tall = center.shape[2]
    for a in range(3):

        def rim(x, carry):
            at = (a * pitch_x + EDGE + x) * pitch_y + 4
            to = pl.ds(pl.multiple_of(x * TALL, 8), TALL)
            stage[0][to, :] = field[pl.ds(at, TALL), :]
            stage[1][to, :] = field[pl.ds(at + (REACH + block_x) * pitch_y, TALL), :]
            return carry

        def middle(x, carry):
            center[a, x] = field[pl.ds((a * pitch_x + HALF + x) * pitch_y, tall), :]
            return carry

        lax.fori_loop(0, REACH, rim, 0, unroll=10)
        lax.fori_loop(0, block_x, middle, 0, unroll=12)
        outgoing(stage, spot[3], row_even, row_odd, a)


def gather_kernel(
    pitch_x, pitch_y, spot, site, posc, own, col_even, col_odd, row_even, row_odd, out, token,
    lattice, wyz, *stages,
):
    col_stage, row_stage = stages[:2], stages[2:]
    hosted = posc.shape[1]
    verts = out.shape[2]
    block_x, block_y = own.shape[1], own.shape[2]
    blank = jnp.zeros((TALL, lattice.shape[1]), F32)

    for a in range(3):
        incoming(col_stage, spot[4], col_even, col_odd, a)
        incoming(row_stage, spot[3], row_even, row_odd, a)

        def inner(x, carry):
            at = (a * pitch_x + HALF + x) * pitch_y
            rim = pl.ds(x * REACH, REACH)
            lattice[pl.ds(at, EDGE), :] = blank[0:EDGE]
            lattice[pl.ds(at + EDGE, REACH), :] = col_stage[0][rim, :]
            lattice[pl.ds(at + HALF, block_y), :] = own[a, x].astype(F32)
            lattice[pl.ds(at + HALF + block_y, REACH), :] = col_stage[1][rim, :]
            lattice[pl.ds(at + HALF + block_y + REACH, EDGE), :] = blank[0:EDGE]
            return carry

        def row_rim(x, carry):
            at = (a * pitch_x + EDGE + x) * pitch_y
            line = pl.ds(pl.multiple_of(x * TALL, 8), TALL)
            lattice[pl.ds(at, TALL), :] = row_stage[0][line, :]
            top = at + (REACH + block_x) * pitch_y
            lattice[pl.ds(top, TALL), :] = row_stage[1][line, :]
            return carry

        lax.fori_loop(0, block_x, inner, 0, unroll=12)
        lax.fori_loop(0, REACH, row_rim, 0, unroll=10)
        for x in (*range(EDGE), *range(pitch_x - EDGE, pitch_x)):
            lattice[pl.ds((a * pitch_x + x) * pitch_y, TALL), :] = blank

    token[...] = jnp.zeros_like(token)
    slot_of = lax.broadcasted_iota(jnp.int32, (3 * BRICK, LANES), 1) // SLOT

    def cell(q, table):
        wx = cell_weights(posc, q, table)
        z0 = site[2, q] - HALF
        first = site[0, q] * pitch_y + site[1, q]
        tiles = []
        for g in range(GROUPS):
            tile = None
            for s in range(PER_TILE):
                lines = jnp.concatenate(
                    [
                        lattice[
                            pl.ds(
                                first + a * pitch_x * pitch_y + PER_TILE * g + s,
                                BRICK,
                                stride=pitch_y,
                            ),
                            :,
                        ]
                        for a in range(3)
                    ],
                    axis=0,
                )
                turned = pltpu.roll(lines, lax.rem(LANES + SLOT * s - z0, LANES), 1)
                tile = turned if tile is None else jnp.where(slot_of == s, turned, tile)
            tiles.append(tile.astype(BF16))
        brick = jnp.concatenate(tiles, axis=1)
        projected = jnp.dot(brick, table[...], preferred_element_type=F32)
        found = jnp.sum(projected.reshape(3, BRICK, -1) * wx[None], axis=1)
        for a in range(3):
            out[a, pl.ds(q, 1), :] = found[a : a + 1, 0:verts]

    def step(t, carry):
        for i in range(TOGETHER):
            cell(TOGETHER * t + i, wyz.at[i])
        return carry

    lax.fori_loop(0, hosted // TOGETHER, step, 0)


def pack_kernel(spot, table, own, out, col_even, col_odd, *stage):
    capacity = out.shape[2]
    block_x, block_y = own.shape[1], own.shape[2]
    for d in range(out.shape[0]):
        for a in range(3):
            out[d, a] = table[a, capacity * d : capacity * (d + 1), :]
    for a in range(3):

        def line(x, carry):
            cells = own[a, x].astype(F32)
            to = pl.ds(x * REACH, REACH)
            stage[0][to, :] = cells[0:REACH]
            stage[1][to, :] = cells[block_y - REACH :]
            return carry

        lax.fori_loop(0, block_x, line, 0, unroll=12)
        outgoing(stage, spot[4], col_even, col_odd, a)


def widen_kernel(spot, own, col_even, col_odd, row_even, row_odd, *stages):
    block_x, block_y = own.shape[1], own.shape[2]
    col_stage, wide = stages[:2], stages[2:]
    for ref in wide:
        ref[...] = jnp.zeros_like(ref)
    for a in range(3):
        incoming(col_stage, spot[4], col_even, col_odd, a)
        for side, first in enumerate((0, block_x - REACH)):

            def line(x, carry):
                at = x * TALL + HALF
                rim = pl.ds((first + x) * REACH, REACH)
                wide[side][pl.ds(at - REACH, REACH), :] = col_stage[0][rim, :]
                wide[side][pl.ds(at, block_y), :] = own[a, first + x].astype(F32)
                wide[side][pl.ds(at + block_y, REACH), :] = col_stage[1][rim, :]
                return carry

            lax.fori_loop(0, REACH, line, 0, unroll=10)
        outgoing(wide, spot[3], row_even, row_odd, a)


def fill_rims(rim, odd, even_in, odd_in, a):
    reached = REACH * TALL
    far = rim.shape[0] - reached
    rim[reached:far, :] = jnp.zeros((far - reached, rim.shape[1]), F32)
    for parity in range(2):

        @pl.when(odd == parity)
        def _():
            rim[(1 - parity) * far : (1 - parity) * far + reached, :] = even_in[a].astype(F32)
            rim[parity * far : parity * far + reached, :] = odd_in[a].astype(F32)


def fold_rims_kernel(spot, center, row_even, row_odd, col_even, col_odd, rim, *stage):
    block_x, tall = center.shape[1], center.shape[2]
    for a in range(3):
        fill_rims(rim, spot[3], row_even, row_odd, a)

        def line(x, carry):
            at = x * TALL
            to = pl.ds(x * REACH, REACH)
            low, high = EDGE, TALL - HALF
            for side, y in enumerate((low, high)):
                stage[side][to, :] = (
                    center[a, x, y + 4 : y + 4 + REACH, :] + rim[pl.ds(at + y, REACH), :]
                )
            return carry

        lax.fori_loop(0, block_x, line, 0, unroll=12)
        outgoing(stage, spot[4], col_even, col_odd, a)


def total_kernel(
    after, spot, center, row_even, row_odd, col_even, col_odd, out, rim, *stage
):
    block_x, block_y = out.shape[1], out.shape[2]
    for a in range(3):
        fill_rims(rim, spot[3], row_even, row_odd, a)
        incoming(stage, spot[4], col_even, col_odd, a)

        def line(x, carry):
            at = pl.ds(x * REACH, REACH)
            body = rim[pl.ds(x * TALL + HALF, block_y), :]
            out[a, x] = center[a, x, pl.ds(HALF + 4, block_y), :] + body
            out[a, x, 0:REACH, :] += stage[0][at, :]
            out[a, x, block_y - REACH :, :] += stage[1][at, :]
            return carry

        lax.fori_loop(0, block_x, line, 0, unroll=12)


def on_device(velocity, host_owner, host_site, vertices, triangles, neighbours):
    columns = lax.axis_size("col")
    capacity = vertices.shape[0] // columns
    verts = vertices.shape[2]
    lanes = padded_to(verts, LANES)
    hosted = host_owner.shape[0]
    block_x, block_y, depth = velocity.shape[1:]
    wide_x, wide_y = block_x + 2 * HALF, block_y + 2 * HALF
    smem = pl.BlockSpec(memory_space=pltpu.SMEM)
    vmem = pl.BlockSpec(memory_space=pltpu.VMEM)
    params = pltpu.CompilerParams(vmem_limit_bytes=VMEM_LIMIT)
    strip = jax.ShapeDtypeStruct((3, block_x * REACH, depth), BF16)
    stage = [pltpu.VMEM((block_x * REACH, depth), F32)] * 2
    long_strip = jax.ShapeDtypeStruct((3, REACH * TALL, depth), BF16)
    long_stage = [pltpu.VMEM((REACH * TALL, depth), F32)] * 2
    rim_stage = pltpu.VMEM((block_x * TALL, depth), F32)

    row, col = lax.axis_index("row"), lax.axis_index("col")
    spot = jnp.stack([row * block_x, col * block_y, 0 * row, row & 1, col & 1]).astype(jnp.int32)
    places = jnp.concatenate([host_site, host_owner.T], axis=0)
    listed = jnp.concatenate([host_site, neighbours], axis=0).T

    packed, col_even, col_odd = pl.pallas_call(
        pack_kernel,
        out_shape=(jax.ShapeDtypeStruct((columns, 3, capacity, verts), F32), strip, strip),
        in_specs=[smem, vmem, vmem],
        out_specs=(vmem,) * 3,
        scratch_shapes=stage,
        compiler_params=params,
        name="pack_vertices",
    )(spot, vertices.transpose(1, 0, 2), velocity)
    near_even, near_odd = exchange(col_even, col_odd, "col")
    arrived = lax.all_to_all(packed, "col", split_axis=0, concat_axis=0, tiled=True)

    tall = block_y + 2 * (HALF + 4)
    field_pitch = tall + 1
    posc, row_even, row_odd, center = pl.pallas_call(
        functools.partial(spread_kernel, wide_x, field_pitch),
        out_shape=(
            jax.ShapeDtypeStruct((9, hosted, lanes), F32),
            long_strip,
            long_strip,
            jax.ShapeDtypeStruct((3, block_x, tall, depth), F32),
        ),
        in_specs=[smem, smem, vmem, vmem, vmem],
        out_specs=(vmem,) * 4,
        scratch_shapes=[
            pltpu.VMEM((3 * wide_x * field_pitch, depth), F32),
            pltpu.VMEM((TOGETHER, SLOT * BRICK, lanes), BF16),
            pltpu.VMEM((3, hosted, lanes), F32),
            *long_stage,
        ],
        compiler_params=params,
        cost_estimate=pl.CostEstimate(
            flops=20_000_000_000, bytes_accessed=60_000_000, transcendentals=0
        ),
        name="spread_forces",
    )(spot, places, listed, triangles, arrived)

    row_even, row_odd, near_even, near_odd = lax.optimization_barrier(
        (row_even, row_odd, near_even, near_odd)
    )
    row_even, row_odd = exchange(row_even, row_odd, "row")
    col_even, col_odd = pl.pallas_call(
        fold_rims_kernel,
        out_shape=(strip, strip),
        in_specs=[smem, vmem, vmem, vmem],
        out_specs=(vmem, vmem),
        scratch_shapes=[rim_stage, *stage],
        compiler_params=params,
        name="fold_rims",
    )(spot, center, row_even, row_odd)
    col_even, col_odd = exchange(col_even, col_odd, "col")

    wide_even, wide_odd = pl.pallas_call(
        widen_kernel,
        out_shape=(long_strip, long_strip),
        in_specs=[smem, vmem, vmem, vmem],
        out_specs=(vmem, vmem),
        scratch_shapes=stage + long_stage,
        compiler_params=params,
        name="widen_rims",
    )(spot, velocity, near_even, near_odd)
    wide_even, wide_odd = exchange(wide_even, wide_odd, "row")

    lattice_pitch = padded_to(wide_y, 8) + 1
    velocities, token = pl.pallas_call(
        functools.partial(gather_kernel, wide_x, lattice_pitch),
        out_shape=(
            jax.ShapeDtypeStruct((3, hosted, verts), F32),
            jax.ShapeDtypeStruct((8, LANES), F32),
        ),
        in_specs=[smem, smem] + [vmem] * 6,
        out_specs=(vmem, vmem),
        scratch_shapes=[
            pltpu.VMEM((3 * wide_x * lattice_pitch, depth), F32),
            pltpu.VMEM((TOGETHER, SLOT * BRICK, lanes), BF16),
            *stage,
            *long_stage,
        ],
        compiler_params=params,
        cost_estimate=pl.CostEstimate(
            flops=10_000_000_000, bytes_accessed=30_000_000, transcendentals=0
        ),
        name="interpolate_velocity",
    )(spot, places, posc, velocity, near_even, near_odd, wide_even, wide_odd)

    force_field = pl.pallas_call(
        total_kernel,
        out_shape=jax.ShapeDtypeStruct((3, block_x, block_y, depth), F32),
        in_specs=[vmem, smem] + [vmem] * 5,
        out_specs=vmem,
        scratch_shapes=[rim_stage, *stage],
        compiler_params=params,
        name="total_force",
    )(token, spot, center, row_even, row_odd, col_even, col_odd)
    return (force_field, velocities.transpose(1, 0, 2))


def solution(mesh):
    return jax.shard_map(
        on_device,
        mesh=mesh,
        in_specs=(
            P(None, "row", "col", None),
            P(("row", "col"), None),
            P(None, ("row", "col")),
            P(("row", "col"), None, None),
            P(),
            P(None, ("row", "col")),
        ),
        out_specs=(P(None, "row", "col", None), P(("row", "col"), None, None)),
        check_vma=False,
    )
```
